32 devices in a mesh: pair: 2 (over core), virt: 16 (over z, y, x).
Axes of the slice: x: 2, y: 2, z: 4, core: 2. Of those that a mesh axis runs over, the one named last changes fastest.
Arguments:
- amplitudes: bfloat16 [512, 32768], P('virt', 'pair'), may hold values from -6 to 6
- integrals: bfloat16 [32768, 32768], P('virt', 'pair'), may hold values from -0.03125 to 0.03125
- cycle_integrals: bfloat16 [16384, 16384], P('pair', 'virt'), may hold values from -0.125 to 0.125
- virt_count: int32 [8], replicated, may hold values from 32 to 64, as said below
Outputs:
- ladder: bfloat16 [512, 32768], P(None, 'virt')
- cycle: bfloat16 [8192, 16384], P('pair', 'virt')
The draws below stay inside these ranges and needn't reach their ends.
Inputs may be any that keep to these rules, and one draw needn't show every extreme that they name: `virt_count`: every irrep keeps at least half of its 64 slots; some irrep has all 64 and some has exactly half.
All inputs are finite; a program needn't handle non-finite values.
Results may differ from the reference program's by a relative error of at most 0.0049.
Values may be sent and summed in bfloat16 or wider, within the bound.
A program may use at most 256 MiB of HBM per device.

```python
import jax
import jax.numpy as jnp
from jax import lax

VH = 64
IRREPS = 8
OI = 16
OJ = 32
P_SIZE = 512
NAB = 32768
IA = 8192
KC = 16384
JB = 16384


def draw_virt_count(key, part):
    key_order, key_values = jax.random.split(jax.random.fold_in(key, 11))
    order = jax.random.permutation(key_order, IRREPS)
    values = jax.random.randint(key_values, (IRREPS,), VH // 2, VH + 1)
    values = jnp.where(order == 0, VH, jnp.where(order == 1, VH // 2, values))
    return values.astype(jnp.int32)


def level_of(stream_key, shape, cuts, low, high):
    def one(position, parts):
        draws = jax.random.uniform(jax.random.fold_in(jax.random.fold_in(stream_key, 6), position), (parts,), jnp.float32, low / len(cuts), high / len(cuts))
        return jnp.repeat(jnp.exp(draws), shape[position] // parts).reshape((-1,) + (1,) * (len(shape) - position - 1))

    gain = one(*cuts[0])
    for cut in cuts[1:]:
        gain = gain * one(*cut)
    return gain


def noise(stream_key, extent, width, reach, shards=(), kind=jnp.bfloat16):
    factor_of = level_of(stream_key, extent, shards, -0.22, 0.18) if shards else 1.0
    result = jax.random.normal(stream_key, extent, jnp.float32) * width * factor_of
    return jnp.minimum(jnp.maximum(result, -reach), reach).astype(kind)


def setup_inputs(seed: int = 0) -> dict:
    arg_keys = jax.random.split(jax.random.key(seed), 5)
    amplitudes = noise(arg_keys[0], (P_SIZE, NAB), 1.0, 6.0, ((0, 16), (1, 2)))
    integrals = noise(arg_keys[1], (NAB, NAB), NAB ** -0.5, 0.03125, ((0, 16), (1, 2)))
    cycle_integrals = noise(arg_keys[2], (KC, JB), (OJ * VH) ** -0.5, 0.125, ((0, 2), (1, 16)))
    virt_count = draw_virt_count(jax.random.fold_in(arg_keys[4], 71), 0)
    return dict(amplitudes=amplitudes, integrals=integrals, cycle_integrals=cycle_integrals, virt_count=virt_count)


def live_slots(virt_count):
    slot_ids = jnp.arange(VH, dtype=jnp.int32)
    return (slot_ids[None, :] < virt_count[:, None]).astype(jnp.float32)


def reference(amplitudes, integrals, cycle_integrals, virt_count):
    live_slot = live_slots(virt_count)
    pair_live = (live_slot[:, :, None] * live_slot[:, None, :]).reshape(NAB)
    masked = amplitudes * pair_live[None, :].astype(jnp.bfloat16)
    masked_wide = masked.astype(jnp.float32)
    row_blocks = integrals.reshape(IRREPS, NAB // IRREPS, NAB)

    def ladder_block(irrep):
        block_rows = lax.dynamic_index_in_dim(row_blocks, irrep, 0, keepdims=False).astype(jnp.float32)
        return lax.dot_general(masked_wide, block_rows, (((1,), (1,)), ((), ())), precision=lax.Precision.HIGHEST)

    ladder_parts = lax.map(ladder_block, jnp.arange(IRREPS, dtype=jnp.int32))
    summed_ladder = jnp.transpose(ladder_parts, (1, 0, 2)).reshape(P_SIZE, NAB)
    ladder = (summed_ladder * pair_live[None, :]).astype(jnp.bfloat16)
    amp_grid = ladder.astype(jnp.float32).reshape(OI, OJ, IRREPS, VH, VH)
    cycle_blocks = cycle_integrals.reshape(OJ, IRREPS, VH, JB)

    def cycle_block(irrep):
        amp_part = lax.dynamic_index_in_dim(amp_grid, irrep, 2, keepdims=False)
        cycle_part = lax.dynamic_index_in_dim(cycle_blocks, irrep, 1, keepdims=False).astype(jnp.float32)
        return jnp.einsum("ikac,kcj->iaj", amp_part, cycle_part, precision=lax.Precision.HIGHEST)

    cycle_parts = lax.map(cycle_block, jnp.arange(IRREPS, dtype=jnp.int32))
    summed = jnp.transpose(cycle_parts, (1, 0, 2, 3)).reshape(IA, JB)
    keep_cols = jnp.tile(live_slot.reshape(IRREPS * VH), OJ)
    cycle = (summed * keep_cols[None, :]).astype(jnp.bfloat16)
    return ladder, cycle
```

```python
import functools

import jax
import jax.numpy as jnp
from jax import lax
from jax.experimental import pallas as pl
from jax.experimental.pallas import tpu as pltpu
from jax.sharding import PartitionSpec as P

VH = 64
OI = 16
OJ = 32
MESH = pl.DeviceIdType.MESH
CHUNK = 1024
PARTS = ((0, 384), (384, 384), (768, 256))


def irrep_sizes(virt_count, irrep_of):
    irrep_ids = jnp.arange(virt_count.shape[0], dtype=jnp.int32)
    return jnp.sum(
        jnp.where(irrep_of[:, None] == irrep_ids[None, :], virt_count[None, :], 0), axis=1
    )


def pair_mask(virt_count, first_pos, length, slot_width):
    position = first_pos + jnp.arange(length, dtype=jnp.int32)
    irrep_of = position // (slot_width * slot_width)
    slot_one = position // slot_width % slot_width
    slot_two = position % slot_width
    irrep_size = irrep_sizes(virt_count, irrep_of)
    return ((slot_one < irrep_size) & (slot_two < irrep_size)).astype(jnp.float32)


def slot_mask(virt_count, first_pos, length, slot_width):
    position = (first_pos + jnp.arange(length, dtype=jnp.int32)) % (
        virt_count.shape[0] * slot_width
    )
    irrep_of = position // slot_width
    slot_ids = position % slot_width
    return (slot_ids < irrep_sizes(virt_count, irrep_of)).astype(jnp.float32)


def bit_reverse(value, bits):
    out = value * 0
    for b in range(bits):
        out = out + ((value >> b) & 1) * (1 << (bits - 1 - b))
    return out


def place_of(device, bits):
    return (device >> 1) & 1, device & 1, bit_reverse(device >> 2, bits - 2)


def bit_orders(bits):
    high = list(range(bits - 1, 1, -1))
    return (high + [0, 1], high + [1, 0], [0, 1] + high)


def merge_rows(x):
    rows = 1
    for s in x.shape[:-1]:
        rows *= s
    if x.shape[-2] % 16:
        return x.astype(jnp.float32).reshape(rows, x.shape[-1]).astype(x.dtype)
    return x.reshape(rows, x.shape[-1])


def barrier(bits, me, pair):
    sem = pltpu.get_barrier_semaphore()
    for b in range(bits):
        pl.semaphore_signal(
            sem, inc=1, device_id={"virt": me ^ (1 << b), "pair": pair}, device_id_type=MESH
        )
    pl.semaphore_signal(
        sem, inc=1, device_id={"virt": me, "pair": 1 - pair}, device_id_type=MESH
    )
    pl.semaphore_wait(sem, bits + 1)


def gather_copy(buf_at, bits, me, pair, send_sem, recv_sem, chunk, part, step):
    order = bit_orders(bits)[part]
    done = order[:step]
    y, x, r = place_of(me, bits)
    high = len([b for b in done if b > 1])
    off, width = PARTS[part]
    at_y = pl.ds(0, 2) if 1 in done else pl.ds(y, 1)
    at_x = pl.ds(0, 2) if 0 in done else pl.ds(x, 1)
    at_r = pl.ds((r >> high) << high, 1 << high)
    region = buf_at(chunk, at_y, at_x, at_r, pl.ds(off, width))
    return pltpu.make_async_remote_copy(
        src_ref=region,
        dst_ref=region,
        send_sem=send_sem.at[chunk, part, step],
        recv_sem=recv_sem.at[chunk, part, step],
        device_id={"virt": me ^ (1 << order[step]), "pair": pair},
        device_id_type=MESH,
    )


def gather_waves(chunks, bits, copy_of, own_ready, use):
    parts = range(len(PARTS))
    lag = 2
    for tick in range(chunks + lag * bits):
        for step in range(bits, -1, -1):
            chunk = tick - lag * step
            if not 0 <= chunk < chunks:
                continue
            if step == 0:
                own_ready(chunk)
            else:
                for part in parts:
                    copy_of(chunk, part, step - 1).wait_recv()
            if step < bits:
                for part in parts:
                    copy_of(chunk, part, step).start()
        chunk = tick - lag * bits
        if 0 <= chunk < chunks:
            use(chunk)
    for chunk in range(chunks):
        for part in parts:
            for step in range(bits):
                copy_of(chunk, part, step).wait_send()


def ladder_kernel(bits, amp_ref, w_ref, out_ref, held, w_buf, acc, away, near,
                  own_sem, w_sem, send_sem, recv_sem, sum_send, sum_recv, fin_send, fin_recv):
    me = lax.axis_index("virt")
    pair = lax.axis_index("pair")
    chunks = held.shape[0]
    slots = w_buf.shape[0]
    tiles, rows, tile = acc.shape
    half = rows // 2
    y, x, r = place_of(me, bits)

    def own_copy(c):
        return pltpu.make_async_copy(
            amp_ref.at[:, pl.ds(c * CHUNK, CHUNK)], held.at[c, y, x, r], own_sem.at[c]
        )

    def w_copy(c):
        return pltpu.make_async_copy(
            w_ref.at[:, pl.ds(c * CHUNK, CHUNK)], w_buf.at[c % slots], w_sem.at[c % slots]
        )

    def buf_at(c, at_y, at_x, at_r, cols):
        return held.at[c, at_y, at_x, at_r, :, cols]

    def copy_of(c, part, step):
        return gather_copy(buf_at, bits, me, pair, send_sem, recv_sem, c, part, step)

    for c in range(chunks):
        own_copy(c).start()
    for c in range(min(slots, chunks)):
        w_copy(c).start()
    barrier(bits, me, pair)

    def sum_copy(n):
        return pltpu.make_async_remote_copy(
            src_ref=away.at[n], dst_ref=near.at[n], send_sem=sum_send.at[n],
            recv_sem=sum_recv.at[n], device_id={"virt": me, "pair": 1 - pair},
            device_id_type=MESH,
        )

    def fin_copy(n):
        region = out_ref.at[n, pair]
        return pltpu.make_async_remote_copy(
            src_ref=region, dst_ref=region, send_sem=fin_send.at[n],
            recv_sem=fin_recv.at[n], device_id={"virt": me, "pair": 1 - pair},
            device_id_type=MESH,
        )

    def use(c):
        w_copy(c).wait()

        @pl.loop(0, tiles)
        def _(n):
            at = pl.ds(pl.multiple_of(n * tile, tile), tile)
            part = lax.dot_general(
                merge_rows(held[c]), w_buf[c % slots, at, :], (((1,), (1,)), ((), ())),
                preferred_element_type=jnp.float32,
            )
            acc[n] = part if c == 0 else acc[n] + part
            if c == chunks - 1:
                away[n] = acc[n, pl.ds(pl.multiple_of((1 - pair) * half, half), half), :]
                sum_copy(n).start()

        if c + slots < chunks:
            w_copy(c + slots).start()

    gather_waves(chunks, bits, copy_of, lambda c: own_copy(c).wait(), use)

    @pl.loop(0, tiles)
    def _(n):
        sum_copy(n).wait()
        total = acc[n, pl.ds(pl.multiple_of(pair * half, half), half), :] + near[n]
        out_ref[n, pair] = total.astype(out_ref.dtype)
        fin_copy(n).start()

    @pl.loop(0, tiles)
    def _(n):
        fin_copy(n).wait()


def cycle_kernel(bits, u_ref, m_ref, out_ref, held, m_buf, away, near, own,
                 own_sem, m_sem, out_sem, send_sem, recv_sem, sum_send, sum_recv):
    me = lax.axis_index("virt")
    pair = lax.axis_index("pair")
    chunks = held.shape[1]
    groups, irreps, rows, cols = away.shape
    per_group = chunks // groups
    a_count = held.shape[5]
    per_irrep = (1 << bits) // irreps
    tile = min(256, cols)
    y, x, r = place_of(me, bits)

    def own_copy(c):
        return pltpu.make_async_copy(u_ref.at[:, c], held.at[:, c, y, x, r], own_sem.at[c])

    def m_copy(h):
        return pltpu.make_async_copy(m_ref.at[:, h], m_buf.at[h], m_sem.at[h])

    def buf_at(c, at_y, at_x, at_r, at_cols):
        return held.at[:, c, at_y, at_x, at_r, :, at_cols]

    def copy_of(c, part, step):
        return gather_copy(buf_at, bits, me, pair, send_sem, recv_sem, c, part, step)

    for c in range(chunks):
        own_copy(c).start()
    for h in range(irreps):
        m_copy(h).start()
    barrier(bits, me, pair)

    def sum_copy(g, h):
        return pltpu.make_async_remote_copy(
            src_ref=away.at[g, h], dst_ref=near.at[g, h], send_sem=sum_send.at[g, h],
            recv_sem=sum_recv.at[g, h], device_id={"virt": me, "pair": 1 - pair},
            device_id_type=MESH,
        )

    def out_copy(g, h, j):
        size = rows // per_group
        return pltpu.make_async_copy(
            near.at[g, h, pl.ds(j * size, size), :],
            out_ref.at[g * per_group + j, h], out_sem.at[g, h, j],
        )

    def finish(g):
        @pl.loop(0, irreps)
        def _(h):
            sum_copy(g, h).wait_recv()
            near[g, h] = (own[h] + near[g, h].astype(jnp.float32)).astype(near.dtype)
            for j in range(per_group):
                out_copy(g, h, j).start()

    def use(c):
        if (c + 1) % per_group:
            return
        g = c // per_group
        if g:
            finish(g - 1)

        @pl.loop(0, irreps)
        def _(h):
            if g == 0:
                m_copy(h).wait()
            pieces = []
            for side in (1 - pair, pair):
                for j in range(per_group):
                    for s in range(per_irrep):
                        py, px, pr = place_of(h * per_irrep + s, bits)
                        pieces.append(held[side, g * per_group + j, py, px, pr])
            left = merge_rows(jnp.stack(pieces))
            for n in range(cols // tile):
                at = pl.ds(n * tile, tile)
                part = jnp.dot(
                    left, merge_rows(m_buf[h, :, :, at]), preferred_element_type=jnp.float32
                )
                away[g, h, :, at] = part[:rows].astype(away.dtype)
                own[h, :, at] = part[rows:]
            sum_copy(g, h).start()

    gather_waves(chunks, bits, copy_of, lambda c: own_copy(c).wait(), use)
    finish(groups - 1)
    for g in range(groups):
        @pl.loop(0, irreps)
        def _(h):
            sum_copy(g, h).wait_send()
            for j in range(per_group):
                out_copy(g, h, j).wait()


def body(amplitudes, integrals, cycle_integrals, virt_count):
    slot_width = VH
    irrep_total = virt_count.shape[0]
    virt_devs = lax.axis_size("virt")
    bits = virt_devs.bit_length() - 1
    pair_devs = lax.axis_size("pair")
    ab_count, cd_count = integrals.shape
    jb_count = cycle_integrals.shape[1]
    p_rows = amplitudes.shape[0]
    p_all = p_rows * virt_devs
    pair = lax.axis_index("pair")
    virt = lax.axis_index("virt")
    dma = pltpu.SemaphoreType.DMA
    any_spec = pl.BlockSpec(memory_space=pl.ANY)
    parts = len(PARTS)
    masked = amplitudes * pair_mask(virt_count, pair * cd_count, cd_count, slot_width)[
        None, :
    ].astype(jnp.bfloat16)
    chunks = cd_count // CHUNK
    tile = min(256, ab_count)
    tiles = ab_count // tile
    half = p_all // 2
    raw = pl.pallas_call(
        functools.partial(ladder_kernel, bits),
        out_shape=jax.ShapeDtypeStruct((tiles, 2, half, tile), jnp.bfloat16),
        in_specs=[any_spec, any_spec],
        out_specs=pl.BlockSpec(memory_space=pltpu.VMEM),
        scratch_shapes=[
            pltpu.VMEM((chunks, 2, 2, virt_devs // 4, p_rows, CHUNK), jnp.bfloat16),
            pltpu.VMEM((3, ab_count, CHUNK), jnp.bfloat16),
            pltpu.VMEM((tiles, p_all, tile), jnp.float32),
            pltpu.VMEM((tiles, half, tile), jnp.float32),
            pltpu.VMEM((tiles, half, tile), jnp.float32),
            dma((chunks,)),
            dma((3,)),
            dma((chunks, parts, bits)),
            dma((chunks, parts, bits)),
            dma((tiles,)),
            dma((tiles,)),
            dma((tiles,)),
            dma((tiles,)),
        ],
        compiler_params=pltpu.CompilerParams(
            collective_id=0, has_side_effects=True, vmem_limit_bytes=56 * 2**20
        ),
        cost_estimate=pl.CostEstimate(
            flops=2 * p_all * ab_count * cd_count,
            bytes_accessed=2 * ab_count * cd_count,
            transcendentals=0,
        ),
        name="ladder",
    )(masked, integrals)
    grid = raw.reshape((tiles,) + (2,) * bits + (p_rows, tile))
    order = tuple(range(bits, 2, -1)) + (1, 2, bits + 1, 0, bits + 2)
    rows = jnp.transpose(grid, order).reshape(p_all, ab_count)
    keep_pairs = pair_mask(virt_count, virt * ab_count, ab_count, slot_width)[None, :]
    ladder = rows * keep_pairs.astype(jnp.bfloat16)

    a_count = ab_count // slot_width
    k_local = OJ // pair_devs
    half_i = OI // 2
    own_k = lax.dynamic_slice_in_dim(
        ladder.reshape(2, half_i, OJ, a_count, slot_width), pair * k_local, k_local, 2
    )
    sent = jnp.transpose(own_k, (0, 1, 3, 2, 4)).reshape(
        2, half_i, a_count, k_local * slot_width
    )
    groups = half_i // 2
    out_rows = half_i // groups * slot_width
    depth = k_local * slot_width
    cycle = pl.pallas_call(
        functools.partial(cycle_kernel, bits),
        out_shape=jax.ShapeDtypeStruct(
            (half_i, irrep_total, slot_width, jb_count), jnp.bfloat16
        ),
        in_specs=[any_spec, any_spec],
        out_specs=any_spec,
        scratch_shapes=[
            pltpu.VMEM((2, half_i, 2, 2, virt_devs // 4, a_count, depth), jnp.bfloat16),
            pltpu.VMEM((irrep_total, k_local, slot_width, jb_count), jnp.bfloat16),
            pltpu.VMEM((groups, irrep_total, out_rows, jb_count), jnp.bfloat16),
            pltpu.VMEM((groups, irrep_total, out_rows, jb_count), jnp.bfloat16),
            pltpu.VMEM((irrep_total, out_rows, jb_count), jnp.float32),
            dma((half_i,)),
            dma((irrep_total,)),
            dma((groups, irrep_total, 2)),
            dma((half_i, parts, bits)),
            dma((half_i, parts, bits)),
            dma((groups, irrep_total)),
            dma((groups, irrep_total)),
        ],
        compiler_params=pltpu.CompilerParams(
            collective_id=1, has_side_effects=True, vmem_limit_bytes=58 * 2**20
        ),
        cost_estimate=pl.CostEstimate(
            flops=2 * OI * irrep_total * slot_width * depth * jb_count,
            bytes_accessed=4 * irrep_total * depth * jb_count,
            transcendentals=0,
        ),
        name="cycle",
    )(sent, cycle_integrals.reshape(k_local, irrep_total, slot_width, jb_count))
    keep_cols = slot_mask(virt_count, virt * jb_count, jb_count, slot_width)[None, :]
    cycle = cycle.reshape(half_i * irrep_total * slot_width, jb_count) * keep_cols.astype(
        jnp.bfloat16
    )
    return (ladder, cycle)


def solution(mesh):
    placed = (P("virt", "pair"), P("virt", "pair"), P("pair", "virt"), P())
    return jax.shard_map(
        body,
        mesh=mesh,
        in_specs=placed,
        out_specs=(P(None, "virt"), P("pair", "virt")),
        check_vma=False,
    )
```

```python
import functools

import jax
import jax.numpy as jnp
from jax import lax
from jax.experimental import pallas as pl
from jax.experimental.pallas import tpu as pltpu
from jax.sharding import PartitionSpec as P

VH = 64
OI = 16
OJ = 32
MESH = pl.DeviceIdType.MESH
CHUNK = 1024
PARTS = ((0, 384), (384, 384), (768, 256))


def irrep_sizes(virt_count, irrep_of):
    irrep_ids = jnp.arange(virt_count.shape[0], dtype=jnp.int32)
    return jnp.sum(
        jnp.where(irrep_of[:, None] == irrep_ids[None, :], virt_count[None, :], 0), axis=1
    )


def slot_mask(virt_count, first_pos, length, slot_width):
    position = (first_pos + jnp.arange(length, dtype=jnp.int32)) % (
        virt_count.shape[0] * slot_width
    )
    irrep_of = position // slot_width
    slot_ids = position % slot_width
    return (slot_ids < irrep_sizes(virt_count, irrep_of)).astype(jnp.float32)


def bit_reverse(value, bits):
    out = value * 0
    for b in range(bits):
        out = out + ((value >> b) & 1) * (1 << (bits - 1 - b))
    return out


def place_of(device, bits):
    return (device >> 1) & 1, device & 1, bit_reverse(device >> 2, bits - 2)


def bit_orders(bits):
    high = list(range(bits - 1, 1, -1))
    return (high + [0, 1], high + [1, 0], [0, 1] + high)


def merge_rows(x):
    rows = 1
    for s in x.shape[:-1]:
        rows *= s
    if x.shape[-2] % 16:
        return x.astype(jnp.float32).reshape(rows, x.shape[-1]).astype(x.dtype)
    return x.reshape(rows, x.shape[-1])


def barrier(bits, me, pair):
    sem = pltpu.get_barrier_semaphore()
    for b in range(bits):
        pl.semaphore_signal(
            sem, inc=1, device_id={"virt": me ^ (1 << b), "pair": pair}, device_id_type=MESH
        )
    pl.semaphore_signal(
        sem, inc=1, device_id={"virt": me, "pair": 1 - pair}, device_id_type=MESH
    )
    pl.semaphore_wait(sem, bits + 1)


def gather_copy(buf_at, bits, me, pair, send_sem, recv_sem, chunk, part, step):
    order = bit_orders(bits)[part]
    done = order[:step]
    y, x, r = place_of(me, bits)
    high = len([b for b in done if b > 1])
    off, width = PARTS[part]
    at_y = pl.ds(0, 2) if 1 in done else pl.ds(y, 1)
    at_x = pl.ds(0, 2) if 0 in done else pl.ds(x, 1)
    at_r = pl.ds((r >> high) << high, 1 << high)
    region = buf_at(chunk, at_y, at_x, at_r, pl.ds(off, width))
    return pltpu.make_async_remote_copy(
        src_ref=region,
        dst_ref=region,
        send_sem=send_sem.at[chunk, part, step],
        recv_sem=recv_sem.at[chunk, part, step],
        device_id={"virt": me ^ (1 << order[step]), "pair": pair},
        device_id_type=MESH,
    )


def gather_waves(chunks, bits, copy_of, own_ready, use):
    parts = range(len(PARTS))
    lag = 2
    for tick in range(chunks + lag * bits):
        due = [(tick - lag * step, step) for step in range(bits, -1, -1)]
        due = [(c, step) for c, step in due if 0 < c < chunks or (c, step) == (0, bits)]
        if tick < bits:
            due.insert(0, (0, tick))
        for chunk, step in due:
            if step == 0:
                own_ready(chunk)
            else:
                for part in parts:
                    copy_of(chunk, part, step - 1).wait_recv()
            if step < bits:
                for part in parts:
                    copy_of(chunk, part, step).start()
        chunk = tick - lag * bits
        if 0 <= chunk < chunks:
            use(chunk)
    for chunk in range(chunks):
        for part in parts:
            for step in range(bits):
                copy_of(chunk, part, step).wait_send()


def live_columns(count_ref, first, width):
    block = VH * VH
    live = count_ref[first // block]
    slot_one = lax.rem(first, block) // VH + lax.broadcasted_iota(jnp.int32, (1, width), 1) // VH
    slot_two = lax.broadcasted_iota(jnp.int32, (1, width), 1) % VH
    return jnp.where((slot_one < live) & (slot_two < live), 1.0, 0.0)


def ladder_kernel(bits, amp_ref, w_ref, count_ref, out_ref, held, w_buf, acc, away, near,
                  own_sem, w_sem, send_sem, recv_sem, sum_send, sum_recv, fin_send, fin_recv):
    me = lax.axis_index("virt")
    pair = lax.axis_index("pair")
    chunks = held.shape[0]
    slots = w_buf.shape[0]
    tiles, rows, tile = acc.shape
    half = rows // 2
    y, x, r = place_of(me, bits)

    def own_copy(c):
        return pltpu.make_async_copy(
            amp_ref.at[:, pl.ds(c * CHUNK, CHUNK)], held.at[c, y, x, r], own_sem.at[c]
        )

    def w_copy(c):
        return pltpu.make_async_copy(
            w_ref.at[:, pl.ds(c * CHUNK, CHUNK)], w_buf.at[c % slots], w_sem.at[c % slots]
        )

    def buf_at(c, at_y, at_x, at_r, cols):
        return held.at[c, at_y, at_x, at_r, :, cols]

    def copy_of(c, part, step):
        return gather_copy(buf_at, bits, me, pair, send_sem, recv_sem, c, part, step)

    for c in range(chunks):
        own_copy(c).start()
    for c in range(min(slots, chunks)):
        w_copy(c).start()
    barrier(bits, me, pair)

    def sum_copy(n):
        return pltpu.make_async_remote_copy(
            src_ref=away.at[n], dst_ref=near.at[n], send_sem=sum_send.at[n],
            recv_sem=sum_recv.at[n], device_id={"virt": me, "pair": 1 - pair},
            device_id_type=MESH,
        )

    def at_tile(n):
        return pl.ds(pl.multiple_of(n * tile, tile), tile)

    def fin_copy(n):
        region = out_ref.at[:, pair, :, :, at_tile(n)]
        return pltpu.make_async_remote_copy(
            src_ref=region, dst_ref=region, send_sem=fin_send.at[n],
            recv_sem=fin_recv.at[n], device_id={"virt": me, "pair": 1 - pair},
            device_id_type=MESH,
        )

    def use(c):
        w_copy(c).wait()

        @pl.loop(0, tiles)
        def _(n):
            part = lax.dot_general(
                merge_rows(held[c]), w_buf[c % slots, at_tile(n), :], (((1,), (1,)), ((), ())),
                preferred_element_type=jnp.float32,
            )
            acc[n] = part if c == 0 else acc[n] + part
            if c == chunks - 1:
                away[n] = acc[n, pl.ds(pl.multiple_of((1 - pair) * half, half), half), :]
                sum_copy(n).start()

        if c + slots < chunks:
            w_copy(c + slots).start()

    def own_ready(c):
        own_copy(c).wait()
        keep = live_columns(count_ref, pair * (chunks * CHUNK) + c * CHUNK, CHUNK)
        held[c, y, x, r] = held[c, y, x, r] * keep.astype(held.dtype)

    gather_waves(chunks, bits, copy_of, own_ready, use)
    fours = held.shape[3]
    p_rows = held.shape[4]

    @pl.loop(0, tiles)
    def _(n):
        sum_copy(n).wait()
        total = acc[n, pl.ds(pl.multiple_of(pair * half, half), half), :] + near[n]
        total = total * live_columns(count_ref, me * (tiles * tile) + n * tile, tile)
        total = total.astype(out_ref.dtype)
        for ox in range(2):
            for o in range(fours):
                first = (ox * fours + o) * p_rows
                out_ref[bit_reverse(o, bits - 2), pair, ox, :, at_tile(n)] = total[
                    first : first + p_rows
                ]
        fin_copy(n).start()

    @pl.loop(0, tiles)
    def _(n):
        fin_copy(n).wait()


def cycle_groups(all_i):
    firsts = list(range(0, all_i - 2, 2))
    return [(f, 2) for f in firsts] + [(all_i - 2, 1), (all_i - 1, 1)]


def cycle_kernel(bits, u_ref, m_ref, out_ref, held, m_buf, away, near, own,
                 own_sem, m_sem, out_sem, send_sem, recv_sem, sum_send, sum_recv):
    me = lax.axis_index("virt")
    pair = lax.axis_index("pair")
    chunks = held.shape[1]
    all_i, irreps, slot_rows, cols = away.shape
    split = chunks // all_i
    groups = cycle_groups(all_i)
    per_irrep = (1 << bits) // irreps
    tile = min(256, cols)
    y, x, r = place_of(me, bits)

    def own_copy(c):
        return pltpu.make_async_copy(u_ref.at[:, c], held.at[:, c, y, x, r], own_sem.at[c])

    def m_copy(h):
        return pltpu.make_async_copy(m_ref.at[:, h], m_buf.at[h], m_sem.at[h])

    def buf_at(c, at_y, at_x, at_r, at_cols):
        return held.at[:, c, at_y, at_x, at_r, :, at_cols]

    def copy_of(c, part, step):
        return gather_copy(buf_at, bits, me, pair, send_sem, recv_sem, c, part, step)

    for c in range(chunks):
        own_copy(c).start()
    for h in range(irreps):
        m_copy(h).start()
    barrier(bits, me, pair)

    def rows_of(ref, g, h):
        return ref.at[pl.ds(groups[g][0], groups[g][1]), h]

    def sum_copy(g, h):
        return pltpu.make_async_remote_copy(
            src_ref=rows_of(away, g, h), dst_ref=rows_of(near, g, h), send_sem=sum_send.at[g, h],
            recv_sem=sum_recv.at[g, h], device_id={"virt": me, "pair": 1 - pair},
            device_id_type=MESH,
        )

    def out_copy(g, h):
        return pltpu.make_async_copy(
            rows_of(near, g, h), rows_of(out_ref, g, h), out_sem.at[g, h]
        )

    def finish(g):
        first, size = groups[g]

        @pl.loop(0, irreps)
        def _(h):
            sum_copy(g, h).wait_recv()
            for j in range(size):
                total = own[h, j] + near[first + j, h].astype(jnp.float32)
                near[first + j, h] = total.astype(near.dtype)
            out_copy(g, h).start()

    def use(c):
        ends = [(first + size) * split - 1 for first, size in groups]
        if c not in ends:
            return
        g = ends.index(c)
        first, size = groups[g]
        if g:
            finish(g - 1)

        @pl.loop(0, irreps)
        def _(h):
            if g == 0:
                m_copy(h).wait()
            pieces = []
            for side in (1 - pair, pair):
                for i in range(first, first + size):
                    for s in range(per_irrep):
                        py, px, pr = place_of(h * per_irrep + s, bits)
                        for k in range(split):
                            pieces.append(held[side, i * split + k, py, px, pr])
            left = merge_rows(jnp.stack(pieces))
            for n in range(cols // tile):
                at = pl.ds(n * tile, tile)
                part = jnp.dot(
                    left, merge_rows(m_buf[h, :, :, at]), preferred_element_type=jnp.float32
                )
                for j in range(size):
                    lo, hi = j * slot_rows, (size + j) * slot_rows
                    away[first + j, h, :, at] = part[lo : lo + slot_rows].astype(away.dtype)
                    own[h, j, :, at] = part[hi : hi + slot_rows]
            sum_copy(g, h).start()

    gather_waves(chunks, bits, copy_of, lambda c: own_copy(c).wait(), use)
    finish(len(groups) - 1)
    for g in range(len(groups)):
        @pl.loop(0, irreps)
        def _(h):
            sum_copy(g, h).wait_send()
            out_copy(g, h).wait()


def body(amplitudes, integrals, cycle_integrals, virt_count):
    slot_width = VH
    irrep_total = virt_count.shape[0]
    virt_devs = lax.axis_size("virt")
    bits = virt_devs.bit_length() - 1
    pair_devs = lax.axis_size("pair")
    ab_count, cd_count = integrals.shape
    jb_count = cycle_integrals.shape[1]
    p_rows = amplitudes.shape[0]
    p_all = p_rows * virt_devs
    pair = lax.axis_index("pair")
    virt = lax.axis_index("virt")
    dma = pltpu.SemaphoreType.DMA
    any_spec = pl.BlockSpec(memory_space=pl.ANY)
    parts = len(PARTS)
    chunks = cd_count // CHUNK
    tile = min(256, ab_count)
    tiles = ab_count // tile
    half = p_all // 2
    raw = pl.pallas_call(
        functools.partial(ladder_kernel, bits),
        out_shape=jax.ShapeDtypeStruct(
            (virt_devs // 4, 2, 2, p_rows, ab_count), jnp.bfloat16
        ),
        in_specs=[any_spec, any_spec, pl.BlockSpec(memory_space=pltpu.SMEM)],
        out_specs=pl.BlockSpec(memory_space=pltpu.VMEM),
        scratch_shapes=[
            pltpu.VMEM((chunks, 2, 2, virt_devs // 4, p_rows, CHUNK), jnp.bfloat16),
            pltpu.VMEM((3, ab_count, CHUNK), jnp.bfloat16),
            pltpu.VMEM((tiles, p_all, tile), jnp.float32),
            pltpu.VMEM((tiles, half, tile), jnp.float32),
            pltpu.VMEM((tiles, half, tile), jnp.float32),
            dma((chunks,)),
            dma((3,)),
            dma((chunks, parts, bits)),
            dma((chunks, parts, bits)),
            dma((tiles,)),
            dma((tiles,)),
            dma((tiles,)),
            dma((tiles,)),
        ],
        compiler_params=pltpu.CompilerParams(
            collective_id=0, has_side_effects=True, vmem_limit_bytes=56 * 2**20
        ),
        cost_estimate=pl.CostEstimate(
            flops=2 * p_all * ab_count * cd_count,
            bytes_accessed=2 * ab_count * cd_count,
            transcendentals=0,
        ),
        name="ladder",
    )(amplitudes, integrals, virt_count)
    ladder = raw.reshape(p_all, ab_count)

    a_count = ab_count // slot_width
    k_local = OJ // pair_devs
    half_i = OI // 2
    own_k = lax.dynamic_slice_in_dim(
        ladder.reshape(2, half_i, OJ, a_count, slot_width), pair * k_local, k_local, 2
    )
    split = 2 if a_count % 32 == 0 else 1
    chunks = half_i * split
    sent = jnp.transpose(own_k, (0, 1, 3, 2, 4)).reshape(
        2, chunks, a_count // split, k_local * slot_width
    )
    groups = len(cycle_groups(half_i))
    depth = k_local * slot_width
    cycle = pl.pallas_call(
        functools.partial(cycle_kernel, bits),
        out_shape=jax.ShapeDtypeStruct(
            (half_i, irrep_total, slot_width, jb_count), jnp.bfloat16
        ),
        in_specs=[any_spec, any_spec],
        out_specs=any_spec,
        scratch_shapes=[
            pltpu.VMEM(
                (2, chunks, 2, 2, virt_devs // 4, a_count // split, depth), jnp.bfloat16
            ),
            pltpu.VMEM((irrep_total, k_local, slot_width, jb_count), jnp.bfloat16),
            pltpu.VMEM((half_i, irrep_total, slot_width, jb_count), jnp.bfloat16),
            pltpu.VMEM((half_i, irrep_total, slot_width, jb_count), jnp.bfloat16),
            pltpu.VMEM((irrep_total, 2, slot_width, jb_count), jnp.float32),
            dma((chunks,)),
            dma((irrep_total,)),
            dma((groups, irrep_total)),
            dma((chunks, parts, bits)),
            dma((chunks, parts, bits)),
            dma((groups, irrep_total)),
            dma((groups, irrep_total)),
        ],
        compiler_params=pltpu.CompilerParams(
            collective_id=1, has_side_effects=True, vmem_limit_bytes=58 * 2**20
        ),
        cost_estimate=pl.CostEstimate(
            flops=2 * OI * irrep_total * slot_width * depth * jb_count,
            bytes_accessed=4 * irrep_total * depth * jb_count,
            transcendentals=0,
        ),
        name="cycle",
    )(sent, cycle_integrals.reshape(k_local, irrep_total, slot_width, jb_count))
    keep_cols = slot_mask(virt_count, virt * jb_count, jb_count, slot_width)[None, :]
    cycle = cycle.reshape(half_i * irrep_total * slot_width, jb_count) * keep_cols.astype(
        jnp.bfloat16
    )
    return (ladder, cycle)


def solution(mesh):
    placed = (P("virt", "pair"), P("virt", "pair"), P("pair", "virt"), P())
    return jax.shard_map(
        body,
        mesh=mesh,
        in_specs=placed,
        out_specs=(P(None, "virt"), P("pair", "virt")),
        check_vma=False,
    )
```

```python
import functools

import jax
import jax.numpy as jnp
from jax import lax
from jax.experimental import pallas as pl
from jax.experimental.pallas import tpu as pltpu
from jax.sharding import PartitionSpec as P

VH = 64
OI = 16
OJ = 32
MESH = pl.DeviceIdType.MESH
CHUNK = 1024
WIDTHS = ((384, 384, 256), (512, 384, 128), (384, 384, 256), (384, 512, 128))


def irrep_sizes(virt_count, irrep_of):
    irrep_ids = jnp.arange(virt_count.shape[0], dtype=jnp.int32)
    return jnp.sum(
        jnp.where(irrep_of[:, None] == irrep_ids[None, :], virt_count[None, :], 0), axis=1
    )


def slot_mask(virt_count, first_pos, length, slot_width):
    position = (first_pos + jnp.arange(length, dtype=jnp.int32)) % (
        virt_count.shape[0] * slot_width
    )
    irrep_of = position // slot_width
    slot_ids = position % slot_width
    return (slot_ids < irrep_sizes(virt_count, irrep_of)).astype(jnp.float32)


def bit_reverse(value, bits):
    out = value * 0
    for b in range(bits):
        out = out + ((value >> b) & 1) * (1 << (bits - 1 - b))
    return out


def place_of(device, bits):
    return (device >> 1) & 1, device & 1, bit_reverse(device >> 2, bits - 2)


def bit_orders(bits):
    high = list(range(bits - 1, 1, -1))
    return (high + [0, 1], high + [1, 0], [0, 1] + high)


def merge_rows(x):
    rows = 1
    for s in x.shape[:-1]:
        rows *= s
    if x.shape[-2] % 16:
        return x.astype(jnp.float32).reshape(rows, x.shape[-1]).astype(x.dtype)
    return x.reshape(rows, x.shape[-1])


def barrier(bits, me, pair):
    sem = pltpu.get_barrier_semaphore()
    for b in range(bits):
        pl.semaphore_signal(
            sem, inc=1, device_id={"virt": me ^ (1 << b), "pair": pair}, device_id_type=MESH
        )
    pl.semaphore_signal(
        sem, inc=1, device_id={"virt": me, "pair": 1 - pair}, device_id_type=MESH
    )
    pl.semaphore_wait(sem, bits + 1)


def gather_copy(buf_at, bits, me, pair, send_sem, recv_sem, chunk, part, step):
    order = bit_orders(bits)[part]
    done = order[:step]
    y, x, r = place_of(me, bits)
    high = len([b for b in done if b > 1])
    widths = WIDTHS[chunk % len(WIDTHS)]
    off, width = sum(widths[:part]), widths[part]
    at_y = pl.ds(0, 2) if 1 in done else pl.ds(y, 1)
    at_x = pl.ds(0, 2) if 0 in done else pl.ds(x, 1)
    at_r = pl.ds((r >> high) << high, 1 << high)
    region = buf_at(chunk, at_y, at_x, at_r, pl.ds(off, width))
    return pltpu.make_async_remote_copy(
        src_ref=region,
        dst_ref=region,
        send_sem=send_sem.at[chunk, part, step],
        recv_sem=recv_sem.at[chunk, part, step],
        device_id={"virt": me ^ (1 << order[step]), "pair": pair},
        device_id_type=MESH,
    )


def gather_waves(chunks, bits, copy_of, own_ready, use):
    parts = range(len(WIDTHS[0]))
    lag = 2
    for tick in range(chunks + lag * bits):
        due = [(tick - lag * step, step) for step in range(bits, -1, -1)]
        due = [(c, step) for c, step in due if 0 < c < chunks or (c, step) == (0, bits)]
        if tick < bits:
            due.insert(0, (0, tick))
        for chunk, step in due:
            if step == 0:
                own_ready(chunk)
            else:
                for part in parts:
                    copy_of(chunk, part, step - 1).wait_recv()
            if step < bits:
                for part in parts:
                    copy_of(chunk, part, step).start()
        chunk = tick - lag * bits
        if 0 <= chunk < chunks:
            use(chunk)
    for chunk in range(chunks):
        for part in parts:
            for step in range(bits):
                copy_of(chunk, part, step).wait_send()


def live_columns(count_ref, first, width):
    block = VH * VH
    live = count_ref[first // block]
    slot_one = lax.rem(first, block) // VH + lax.broadcasted_iota(jnp.int32, (1, width), 1) // VH
    slot_two = lax.broadcasted_iota(jnp.int32, (1, width), 1) % VH
    return jnp.where((slot_one < live) & (slot_two < live), 1.0, 0.0)


def ladder_kernel(bits, amp_ref, w_ref, count_ref, out_ref, held, w_buf, acc, away, near,
                  own_sem, w_sem, send_sem, recv_sem, sum_send, sum_recv, fin_send, fin_recv):
    me = lax.axis_index("virt")
    pair = lax.axis_index("pair")
    chunks = held.shape[0]
    slots = w_buf.shape[0]
    tiles, rows, tile = acc.shape
    half = rows // 2
    y, x, r = place_of(me, bits)

    def own_copy(c):
        return pltpu.make_async_copy(
            amp_ref.at[:, pl.ds(c * CHUNK, CHUNK)], held.at[c, y, x, r], own_sem.at[c]
        )

    def w_copy(c):
        return pltpu.make_async_copy(
            w_ref.at[:, pl.ds(c * CHUNK, CHUNK)], w_buf.at[c % slots], w_sem.at[c % slots]
        )

    def buf_at(c, at_y, at_x, at_r, cols):
        return held.at[c, at_y, at_x, at_r, :, cols]

    def copy_of(c, part, step):
        return gather_copy(buf_at, bits, me, pair, send_sem, recv_sem, c, part, step)

    for c in range(chunks):
        own_copy(c).start()
    for c in range(min(slots, chunks)):
        w_copy(c).start()
    barrier(bits, me, pair)

    def sum_copy(n):
        return pltpu.make_async_remote_copy(
            src_ref=away.at[n], dst_ref=near.at[n], send_sem=sum_send.at[n],
            recv_sem=sum_recv.at[n], device_id={"virt": me, "pair": 1 - pair},
            device_id_type=MESH,
        )

    def at_tile(n):
        return pl.ds(pl.multiple_of(n * tile, tile), tile)

    def fin_copy(n):
        region = out_ref.at[:, pair, :, :, at_tile(n)]
        return pltpu.make_async_remote_copy(
            src_ref=region, dst_ref=region, send_sem=fin_send.at[n],
            recv_sem=fin_recv.at[n], device_id={"virt": me, "pair": 1 - pair},
            device_id_type=MESH,
        )

    def use(c):
        w_copy(c).wait()

        @pl.loop(0, tiles)
        def _(n):
            part = lax.dot_general(
                merge_rows(held[c]), w_buf[c % slots, at_tile(n), :], (((1,), (1,)), ((), ())),
                preferred_element_type=jnp.float32,
            )
            acc[n] = part if c == 0 else acc[n] + part
            if c == chunks - 1:
                away[n] = acc[n, pl.ds(pl.multiple_of((1 - pair) * half, half), half), :]
                sum_copy(n).start()

        if c + slots < chunks:
            w_copy(c + slots).start()

    def own_ready(c):
        own_copy(c).wait()
        keep = live_columns(count_ref, pair * (chunks * CHUNK) + c * CHUNK, CHUNK)
        held[c, y, x, r] = held[c, y, x, r] * keep.astype(held.dtype)

    gather_waves(chunks, bits, copy_of, own_ready, use)
    fours = held.shape[3]
    p_rows = held.shape[4]

    @pl.loop(0, tiles)
    def _(n):
        sum_copy(n).wait()
        total = acc[n, pl.ds(pl.multiple_of(pair * half, half), half), :] + near[n]
        total = total * live_columns(count_ref, me * (tiles * tile) + n * tile, tile)
        total = total.astype(out_ref.dtype)
        for ox in range(2):
            for o in range(fours):
                first = (ox * fours + o) * p_rows
                out_ref[bit_reverse(o, bits - 2), pair, ox, :, at_tile(n)] = total[
                    first : first + p_rows
                ]
        fin_copy(n).start()

    @pl.loop(0, tiles)
    def _(n):
        fin_copy(n).wait()


def cycle_groups(all_i):
    firsts = list(range(0, all_i - 2, 2))
    return [(f, 2) for f in firsts] + [(all_i - 2, 1), (all_i - 1, 1)]


def cycle_kernel(bits, u_ref, m_ref, out_ref, held, m_buf, away, near, own,
                 own_sem, m_sem, out_sem, send_sem, recv_sem, sum_send, sum_recv):
    me = lax.axis_index("virt")
    pair = lax.axis_index("pair")
    chunks = held.shape[1]
    all_i, irreps, slot_rows, cols = away.shape
    split = chunks // all_i
    groups = cycle_groups(all_i)
    per_irrep = (1 << bits) // irreps
    tile = min(256, cols)
    y, x, r = place_of(me, bits)

    def own_copy(c):
        return pltpu.make_async_copy(u_ref.at[:, c], held.at[:, c, y, x, r], own_sem.at[c])

    def m_copy(h):
        return pltpu.make_async_copy(m_ref.at[:, h], m_buf.at[h], m_sem.at[h])

    def buf_at(c, at_y, at_x, at_r, at_cols):
        return held.at[:, c, at_y, at_x, at_r, :, at_cols]

    def copy_of(c, part, step):
        return gather_copy(buf_at, bits, me, pair, send_sem, recv_sem, c, part, step)

    for c in range(chunks):
        own_copy(c).start()
    for h in range(irreps):
        m_copy(h).start()
    barrier(bits, me, pair)

    def rows_of(ref, g, h):
        return ref.at[pl.ds(groups[g][0], groups[g][1]), h]

    def sum_copy(g, h):
        return pltpu.make_async_remote_copy(
            src_ref=rows_of(away, g, h), dst_ref=rows_of(near, g, h), send_sem=sum_send.at[g, h],
            recv_sem=sum_recv.at[g, h], device_id={"virt": me, "pair": 1 - pair},
            device_id_type=MESH,
        )

    def out_copy(g, h):
        return pltpu.make_async_copy(
            rows_of(near, g, h), rows_of(out_ref, g, h), out_sem.at[g, h]
        )

    def finish(g):
        first, size = groups[g]

        @pl.loop(0, irreps)
        def _(h):
            sum_copy(g, h).wait_recv()
            for j in range(size):
                total = own[h, j] + near[first + j, h].astype(jnp.float32)
                near[first + j, h] = total.astype(near.dtype)
            out_copy(g, h).start()

    def use(c):
        ends = [(first + size) * split - 1 for first, size in groups]
        if c not in ends:
            return
        g = ends.index(c)
        first, size = groups[g]
        if g:
            finish(g - 1)

        @pl.loop(0, irreps)
        def _(h):
            if g == 0:
                m_copy(h).wait()
            pieces = []
            for side in (1 - pair, pair):
                for i in range(first, first + size):
                    for s in range(per_irrep):
                        py, px, pr = place_of(h * per_irrep + s, bits)
                        for k in range(split):
                            pieces.append(held[side, i * split + k, py, px, pr])
            left = merge_rows(jnp.stack(pieces))
            for n in range(cols // tile):
                at = pl.ds(n * tile, tile)
                part = jnp.dot(
                    left, merge_rows(m_buf[h, :, :, at]), preferred_element_type=jnp.float32
                )
                for j in range(size):
                    lo, hi = j * slot_rows, (size + j) * slot_rows
                    away[first + j, h, :, at] = part[lo : lo + slot_rows].astype(away.dtype)
                    own[h, j, :, at] = part[hi : hi + slot_rows]
            sum_copy(g, h).start()

    gather_waves(chunks, bits, copy_of, lambda c: own_copy(c).wait(), use)
    finish(len(groups) - 1)
    for g in range(len(groups)):
        @pl.loop(0, irreps)
        def _(h):
            sum_copy(g, h).wait_send()
            out_copy(g, h).wait()


def body(amplitudes, integrals, cycle_integrals, virt_count):
    slot_width = VH
    irrep_total = virt_count.shape[0]
    virt_devs = lax.axis_size("virt")
    bits = virt_devs.bit_length() - 1
    pair_devs = lax.axis_size("pair")
    ab_count, cd_count = integrals.shape
    jb_count = cycle_integrals.shape[1]
    p_rows = amplitudes.shape[0]
    p_all = p_rows * virt_devs
    pair = lax.axis_index("pair")
    virt = lax.axis_index("virt")
    dma = pltpu.SemaphoreType.DMA
    any_spec = pl.BlockSpec(memory_space=pl.ANY)
    parts = len(WIDTHS[0])
    chunks = cd_count // CHUNK
    tile = min(256, ab_count)
    tiles = ab_count // tile
    half = p_all // 2
    raw = pl.pallas_call(
        functools.partial(ladder_kernel, bits),
        out_shape=jax.ShapeDtypeStruct(
            (virt_devs // 4, 2, 2, p_rows, ab_count), jnp.bfloat16
        ),
        in_specs=[any_spec, any_spec, pl.BlockSpec(memory_space=pltpu.SMEM)],
        out_specs=pl.BlockSpec(memory_space=pltpu.VMEM),
        scratch_shapes=[
            pltpu.VMEM((chunks, 2, 2, virt_devs // 4, p_rows, CHUNK), jnp.bfloat16),
            pltpu.VMEM((3, ab_count, CHUNK), jnp.bfloat16),
            pltpu.VMEM((tiles, p_all, tile), jnp.float32),
            pltpu.VMEM((tiles, half, tile), jnp.float32),
            pltpu.VMEM((tiles, half, tile), jnp.float32),
            dma((chunks,)),
            dma((3,)),
            dma((chunks, parts, bits)),
            dma((chunks, parts, bits)),
            dma((tiles,)),
            dma((tiles,)),
            dma((tiles,)),
            dma((tiles,)),
        ],
        compiler_params=pltpu.CompilerParams(
            collective_id=0, has_side_effects=True, vmem_limit_bytes=56 * 2**20
        ),
        cost_estimate=pl.CostEstimate(
            flops=2 * p_all * ab_count * cd_count,
            bytes_accessed=2 * ab_count * cd_count,
            transcendentals=0,
        ),
        name="ladder",
    )(amplitudes, integrals, virt_count)
    ladder = raw.reshape(p_all, ab_count)

    a_count = ab_count // slot_width
    k_local = OJ // pair_devs
    half_i = OI // 2
    own_k = lax.dynamic_slice_in_dim(
        ladder.reshape(2, half_i, OJ, ab_count), pair * k_local, k_local, 2
    )
    own_k = lax.optimization_barrier(own_k).reshape(
        2, half_i, k_local, a_count, slot_width
    )
    split = 2 if a_count % 32 == 0 else 1
    chunks = half_i * split
    sent = jnp.transpose(own_k, (0, 1, 3, 2, 4)).reshape(
        2, chunks, a_count // split, k_local * slot_width
    )
    groups = len(cycle_groups(half_i))
    depth = k_local * slot_width
    cycle = pl.pallas_call(
        functools.partial(cycle_kernel, bits),
        out_shape=jax.ShapeDtypeStruct(
            (half_i, irrep_total, slot_width, jb_count), jnp.bfloat16
        ),
        in_specs=[any_spec, any_spec],
        out_specs=any_spec,
        scratch_shapes=[
            pltpu.VMEM(
                (2, chunks, 2, 2, virt_devs // 4, a_count // split, depth), jnp.bfloat16
            ),
            pltpu.VMEM((irrep_total, k_local, slot_width, jb_count), jnp.bfloat16),
            pltpu.VMEM((half_i, irrep_total, slot_width, jb_count), jnp.bfloat16),
            pltpu.VMEM((half_i, irrep_total, slot_width, jb_count), jnp.bfloat16),
            pltpu.VMEM((irrep_total, 2, slot_width, jb_count), jnp.float32),
            dma((chunks,)),
            dma((irrep_total,)),
            dma((groups, irrep_total)),
            dma((chunks, parts, bits)),
            dma((chunks, parts, bits)),
            dma((groups, irrep_total)),
            dma((groups, irrep_total)),
        ],
        compiler_params=pltpu.CompilerParams(
            collective_id=1, has_side_effects=True, vmem_limit_bytes=58 * 2**20
        ),
        cost_estimate=pl.CostEstimate(
            flops=2 * OI * irrep_total * slot_width * depth * jb_count,
            bytes_accessed=4 * irrep_total * depth * jb_count,
            transcendentals=0,
        ),
        name="cycle",
    )(sent, cycle_integrals.reshape(k_local, irrep_total, slot_width, jb_count))
    keep_cols = slot_mask(virt_count, virt * jb_count, jb_count, slot_width)[None, :]
    cycle = cycle.reshape(half_i * irrep_total * slot_width, jb_count) * keep_cols.astype(
        jnp.bfloat16
    )
    return (ladder, cycle)


def solution(mesh):
    placed = (P("virt", "pair"), P("virt", "pair"), P("pair", "virt"), P())
    return jax.shard_map(
        body,
        mesh=mesh,
        in_specs=placed,
        out_specs=(P(None, "virt"), P("pair", "virt")),
        check_vma=False,
    )
```
